32 devices in a mesh: tm: 8 (over y, x, core), patch: 4 (over z).
Axes of the slice: x: 2, y: 2, z: 4, core: 2. Of those that a mesh axis runs over, the one named last changes fastest.
Arguments:
- frames_in: bfloat16 [64, 256, 1024], P('tm', 'patch'), may hold values from -6 to 6
- codes: int32 [64, 256], P('tm', 'patch'), may hold values from 0 to 1023
- gain_space: float32 [1024], replicated, may hold values from 0.1 to 1.9
- qkv_space: bfloat16 [1024, 3072], replicated, may hold values from -0.1875 to 0.1875
- out_space: bfloat16 [1024, 1024], replicated, may hold values from -0.75 to 0.75
- scale_space: float32 [16], replicated, may hold values from 3 to 12
- gain_time: float32 [1024], replicated, may hold values from 0.1 to 1.9
- qkv_time: bfloat16 [1024, 3072], replicated, may hold values from -0.1875 to 0.1875
- out_time: bfloat16 [1024, 1024], replicated, may hold values from -0.75 to 0.75
- scale_time: float32 [16], replicated, may hold values from 3 to 12
- codebook: bfloat16 [1024, 1024], replicated, may hold values from -6 to 6
Outputs:
- encoded: bfloat16 [64, 256, 1024], P('tm', 'patch')
- commitment: bfloat16 [64, 256, 1024], P('tm', 'patch')
The draws below stay inside these ranges and needn't reach their ends.
All inputs are finite; a program needn't handle non-finite values.
Results may differ from the reference program's by a relative error of at most 0.02.
Values may be sent and summed in bfloat16 or wider, within the bound.
A program may use at most 192 MiB of HBM per device.

```python
import math
import jax
import jax.numpy as jnp
from jax import lax

D = 1024
H = 16
HD = 64
CODES = 1024
F = 64
P_SIZE = 256


def plant(values, own_key, low, largest):
    extent = values.shape
    index_at = [jax.random.randint(jax.random.fold_in(own_key, axis), (), 0, extent[axis]) for axis in range(len(extent))]
    values = values.at[tuple(index_at)].set(low)
    longest = extent.index(max(extent))
    index_at[longest] = (index_at[longest] + 1) % extent[longest]
    return values.at[tuple(index_at)].set(largest)


def block_levels(own_key, shape, split, smallest, top_value):
    def one(position, shards_of):
        steps = jax.random.uniform(jax.random.fold_in(jax.random.fold_in(own_key, 6), position), (shards_of,), jnp.float32, smallest / len(split), top_value / len(split))
        return jnp.repeat(jnp.exp(steps), shape[position] // shards_of).reshape((-1,) + (1,) * (len(shape) - position - 1))

    level = one(*split[0])
    for cut in split[1:]:
        level = level * one(*cut)
    return level


def centred(key, dims, width, reach, pieces=(), kind=jnp.bfloat16):
    array = jax.random.normal(key, dims, jnp.float32) * width
    if len(pieces) > 0:
        array = block_levels(key, dims, pieces, -0.22, 0.18) * array
    return jnp.clip(array, min=-reach, max=reach).astype(kind)


def setup_inputs(seed: int = 0) -> dict:
    key_of = jax.random.split(jax.random.key(seed), 12)
    frames_in = centred(key_of[0], (F, P_SIZE, D), 1.0, 6.0, ((0, 8), (1, 4)))
    codes = plant(jax.random.randint(key_of[1], (F, P_SIZE), 0, CODES), jax.random.fold_in(key_of[1], 1), 0, CODES - 1).astype(jnp.int32)
    gain_space = jnp.clip(1.0 + 0.18 * jax.random.normal(key_of[2], (D,), jnp.float32), 0.1, 1.9)
    qkv_space = centred(key_of[3], (D, 3 * D), D ** -0.5, 0.1875)
    out_space = centred(key_of[4], (D, D), (D // 16) ** -0.5, 0.75)
    scale_space = jnp.clip(jnp.exp(jax.random.uniform(key_of[5], (H,), jnp.float32, math.log(3.0), math.log(12.0))), 3.0, 12.0)
    gain_time = jnp.clip(1.0 + 0.18 * jax.random.normal(key_of[6], (D,), jnp.float32), 0.1, 1.9)
    qkv_time = centred(key_of[7], (D, 3 * D), D ** -0.5, 0.1875)
    out_time = centred(key_of[8], (D, D), (D // 16) ** -0.5, 0.75)
    scale_time = jnp.clip(jnp.exp(jax.random.uniform(key_of[9], (H,), jnp.float32, math.log(3.0), math.log(12.0))), 3.0, 12.0)
    codebook = centred(key_of[10], (CODES, D), 1.0, 6.0)
    return dict(frames_in=frames_in, codes=codes, gain_space=gain_space, qkv_space=qkv_space, out_space=out_space, scale_space=scale_space, gain_time=gain_time, qkv_time=qkv_time, out_time=out_time, scale_time=scale_time, codebook=codebook)


def norm_rows(stream, gain):
    wide = stream.astype(jnp.float32)
    return (wide * lax.rsqrt(lax.optimization_barrier(jnp.mean(wide * wide, -1, keepdims=True)) + 1e-05) * gain).astype(jnp.bfloat16)

def project(stream, gain, weights, scale):
    normed = norm_rows(stream, gain)
    lead = normed.shape[:-1]
    qkv = jnp.dot(normed.reshape(-1, D), weights, preferred_element_type=jnp.float32)
    query = qkv[:, :D].reshape(-1, H, HD)
    key = qkv[:, D:2 * D].reshape(-1, H, HD)
    value = qkv[:, 2 * D:]
    query = query * lax.rsqrt(lax.optimization_barrier(jnp.mean(query * query, -1, keepdims=True)) + 1e-06) * (scale[:, None] / HD)
    key = key * lax.rsqrt(lax.optimization_barrier(jnp.mean(key * key, -1, keepdims=True)) + 1e-06)
    return (query.reshape(lead + (D,)).astype(jnp.bfloat16), key.reshape(lead + (D,)).astype(jnp.bfloat16), value.reshape(lead + (D,)).astype(jnp.bfloat16))

def frame_attend(items):
    query, key, value = items
    count = query.shape[0]
    query = query.reshape(count, H, HD).astype(jnp.float32)
    key = key.reshape(count, H, HD).astype(jnp.float32)
    value = value.reshape(count, H, HD).astype(jnp.float32)
    scores = jnp.einsum('phd,qhd->hpq', query, key)
    weight = jnp.exp(scores).astype(jnp.bfloat16).astype(jnp.float32)
    total = jnp.einsum('hpq,qhd->phd', weight, value)
    denom = lax.optimization_barrier(jnp.sum(weight, -1)).T
    return (total / denom[:, :, None]).reshape(count, D).astype(jnp.bfloat16)

def reference(frames_in, codes, gain_space, qkv_space, out_space, scale_space, gain_time, qkv_time, out_time, scale_time, codebook):
    query, key, value = project(frames_in, gain_space, qkv_space, scale_space)
    attn_s = lax.map(frame_attend, (query, key, value))
    stream = frames_in.astype(jnp.float32) + jnp.dot(attn_s.reshape(-1, D), out_space, preferred_element_type=jnp.float32).reshape(F, P_SIZE, D)
    query, key, value = project(stream, gain_time, qkv_time, scale_time)
    query = query.reshape(F, P_SIZE, H, HD).astype(jnp.float32)
    key = key.reshape(F, P_SIZE, H, HD).astype(jnp.float32)
    value = value.reshape(F, P_SIZE, H, HD).astype(jnp.float32)
    scores = jnp.einsum('fphd,gphd->phfg', query, key)
    frame_ids = jnp.arange(F, dtype=jnp.int32)
    causal = frame_ids[:, None] >= frame_ids[None, :]
    weight = jnp.where(causal, jnp.exp(scores), 0.0).astype(jnp.bfloat16).astype(jnp.float32)
    total = jnp.einsum('phfg,gphd->fphd', weight, value)
    denom = jnp.transpose(lax.optimization_barrier(jnp.sum(weight, -1)), (2, 0, 1))
    attn_t = (total / denom[..., None]).reshape(F * P_SIZE, D).astype(jnp.bfloat16)
    output = stream + jnp.dot(attn_t, out_time, preferred_element_type=jnp.float32).reshape(F, P_SIZE, D)
    chosen = jnp.take(codebook, codes, axis=0).astype(jnp.float32)
    return (output.astype(jnp.bfloat16), (output - chosen).astype(jnp.bfloat16))
```

```python
import jax
import jax.numpy as jnp
from jax import lax
from jax.sharding import PartitionSpec as P

H = 16
HD = 64


def norm_rows(stream, gain):
    wide = stream.astype(jnp.float32)
    return (wide * lax.rsqrt(jnp.mean(wide * wide, -1, keepdims=True) + 1e-05) * gain).astype(
        jnp.bfloat16
    )


def project(stream, gain, weights, scale):
    width = stream.shape[-1]
    head_size = width // H
    normed = norm_rows(stream, gain)
    lead = normed.shape[:-1]
    qkv = jnp.dot(normed.reshape(-1, width), weights, preferred_element_type=jnp.float32)
    query = qkv[:, :width].reshape(-1, H, head_size)
    key = qkv[:, width : 2 * width].reshape(-1, H, head_size)
    value = qkv[:, 2 * width :]
    query = (
        query
        * lax.rsqrt(jnp.mean(query * query, -1, keepdims=True) + 1e-06)
        * (scale[:, None] / head_size)
    )
    key = key * lax.rsqrt(jnp.mean(key * key, -1, keepdims=True) + 1e-06)
    return (
        query.reshape(lead + (width,)).astype(jnp.bfloat16),
        key.reshape(lead + (width,)).astype(jnp.bfloat16),
        value.reshape(lead + (width,)).astype(jnp.bfloat16),
    )


def group_lanes(array):
    batch, count, width = array.shape
    lanes = 128
    return jnp.transpose(array.reshape(batch, count, width // lanes, lanes), (0, 2, 1, 3))


def merge_lanes(array):
    batch, groups, count, lanes = array.shape
    return jnp.transpose(array, (0, 2, 1, 3)).reshape(batch, count, groups * lanes)


def head_terms(query, key, value, allowed):
    lanes = query.shape[-1]
    heads = lanes // HD
    lane_head = jnp.arange(lanes, dtype=jnp.int32) // HD
    out_shape = query.shape[:3] + (lanes,)
    total = jnp.zeros(out_shape, jnp.float32)
    denom = jnp.ones(out_shape, jnp.float32)
    for head in range(heads):
        picked = lane_head == head
        masked = jnp.where(picked, query, jnp.zeros_like(query))
        scores = jnp.einsum("bjnc,bjmc->bjnm", masked, key, preferred_element_type=jnp.float32)
        weight = jnp.exp(scores)
        if allowed is not None:
            weight = jnp.where(allowed, weight, 0.0)
        weight = weight.astype(jnp.bfloat16)
        part = jnp.einsum("bjnm,bjmc->bjnc", weight, value, preferred_element_type=jnp.float32)
        total = jnp.where(picked, part, total)
        denom = jnp.where(picked, jnp.sum(weight.astype(jnp.float32), -1)[..., None], denom)
    return (total, denom)


def shards(
    frames_in,
    codes,
    gain_space,
    qkv_space,
    out_space,
    scale_space,
    gain_time,
    qkv_time,
    out_time,
    scale_time,
    codebook,
):
    f_local, p_local, width = frames_in.shape
    own = lax.all_to_all(frames_in, "patch", split_axis=0, concat_axis=1, tiled=True)
    query, key, value = project(own, gain_space, qkv_space, scale_space)
    total, denom = head_terms(group_lanes(query), group_lanes(key), group_lanes(value), None)
    attn_s = merge_lanes(total / denom).astype(jnp.bfloat16)
    stream = own.astype(jnp.float32) + jnp.dot(
        attn_s.reshape(-1, width), out_space, preferred_element_type=jnp.float32
    ).reshape(own.shape)
    stream = stream.astype(jnp.bfloat16)
    stream = lax.all_to_all(stream, "patch", split_axis=1, concat_axis=0, tiled=True)
    stream = lax.all_to_all(stream, "tm", split_axis=1, concat_axis=0, tiled=True)
    stream = jnp.transpose(stream, (1, 0, 2))
    query, key, value = project(stream, gain_time, qkv_time, scale_time)
    order = jnp.arange(stream.shape[1], dtype=jnp.int32)
    allowed = order[:, None] >= order[None, :]
    part, part_denom = head_terms(
        group_lanes(query), group_lanes(key), group_lanes(value), allowed
    )
    attn_t = merge_lanes(part / part_denom).reshape(-1, width).astype(jnp.bfloat16)
    output = stream.astype(jnp.float32) + jnp.dot(
        attn_t, out_time, preferred_element_type=jnp.float32
    ).reshape(stream.shape)
    output = jnp.transpose(output.astype(jnp.bfloat16), (1, 0, 2))
    output = lax.all_to_all(output, "tm", split_axis=0, concat_axis=1, tiled=True)
    code_count = codebook.shape[0]
    one_hot = (codes[..., None] == jnp.arange(code_count, dtype=jnp.int32)).astype(jnp.bfloat16)
    chosen = jnp.dot(
        one_hot.reshape(-1, code_count), codebook, preferred_element_type=jnp.float32
    ).reshape(f_local, p_local, width)
    return (output, (output.astype(jnp.float32) - chosen).astype(jnp.bfloat16))


def solution(mesh):
    return jax.shard_map(
        shards,
        mesh=mesh,
        in_specs=(
            P("tm", "patch", None),
            P("tm", "patch"),
            P(),
            P(),
            P(),
            P(),
            P(),
            P(),
            P(),
            P(),
            P(),
        ),
        out_specs=(P("tm", "patch", None), P("tm", "patch", None)),
        check_vma=False,
    )
```

```python
import functools

import jax
import jax.numpy as jnp
from jax import lax
from jax.experimental import pallas as pl
from jax.experimental.pallas import tpu as pltpu
from jax.sharding import PartitionSpec as P

HD = 64
LANES = 256
PACK = 16
MESH = pl.DeviceIdType.MESH


def lane_heads(rows):
    return lax.broadcasted_iota(jnp.int32, (rows, LANES), 1) // HD


def attend(x, gain, qkv_ref, out_ref, scale_ref, allowed, normed, attn):
    count, width = x.shape
    heads = LANES // HD
    square = jnp.mean(x * x, -1, keepdims=True)
    normed[...] = (x * lax.rsqrt(square + 1e-05) * gain).astype(jnp.bfloat16)
    lane_head = lane_heads(1)
    own_head = lax.broadcasted_iota(jnp.int32, (LANES, LANES), 0) // HD == lane_heads(LANES)
    head_mean = jnp.where(own_head, 1.0 / HD, 0.0).astype(jnp.bfloat16)
    rows_head = lax.broadcasted_iota(jnp.int32, (heads * count, LANES), 0) // count
    head_sum = jnp.where(rows_head == lane_heads(heads * count), 1.0, 0.0).astype(jnp.bfloat16)

    def unit(part):
        mean = jnp.dot(
            (part * part).astype(jnp.bfloat16), head_mean, preferred_element_type=jnp.float32
        )
        return part * lax.rsqrt(mean + 1e-06)

    def group(g, carry):
        def project(block):
            columns = pl.ds(pl.multiple_of(block * width + g * LANES, LANES), LANES)
            return jnp.dot(normed[...], qkv_ref[:, columns], preferred_element_type=jnp.float32)

        scale = jnp.zeros((1, LANES), jnp.float32)
        for h in range(heads):
            scale = jnp.where(lane_head == h, scale_ref[g * heads + h], scale)
        query = unit(project(0)) * (scale * (1.0 / HD))
        key = unit(project(1)).astype(jnp.bfloat16)
        value = project(2)
        stacked = jnp.concatenate(
            [jnp.where(lane_head == h, query, 0.0).astype(jnp.bfloat16) for h in range(heads)], 0
        )
        values = jnp.concatenate(
            [jnp.where(lane_head == h, value, 0.0).astype(jnp.bfloat16) for h in range(heads)], 0
        )
        scores = lax.dot_general(
            stacked, key, (((1,), (1,)), ((), ())), preferred_element_type=jnp.float32
        )
        weights = []
        for h in range(heads):
            weight = jnp.exp(scores[h * count : (h + 1) * count])
            if allowed is not None:
                weight = jnp.where(allowed, weight, 0.0)
            weights.append(weight.astype(jnp.bfloat16))
        weight = jnp.concatenate(weights, 1)
        total = jnp.dot(weight, values, preferred_element_type=jnp.float32)
        denom = jnp.dot(weight, head_sum, preferred_element_type=jnp.float32)
        columns = pl.ds(pl.multiple_of(g * LANES, LANES), LANES)
        attn[:, columns] = (total / denom).astype(jnp.bfloat16)
        return carry

    lax.fori_loop(0, width // LANES, group, 0)
    return x + jnp.dot(attn[...], out_ref[...], preferred_element_type=jnp.float32)


def kernel(
    n_tm,
    n_patch,
    x_hbm,
    codes_ref,
    gain_space,
    qkv_space_hbm,
    out_space_hbm,
    scale_space,
    gain_time,
    qkv_time_hbm,
    out_time_hbm,
    scale_time,
    codebook_hbm,
    encoded,
    commitment,
    qkv_space,
    out_space,
    qkv_time,
    out_time,
    codebook,
    whole,
    packed,
    arrived,
    wide,
    leaving,
    landed,
    chosen,
    normed_s,
    attn_s,
    normed_t,
    attn_t,
    load_sem,
    in_send,
    in_recv,
    mid_send,
    mid_recv,
    out_send,
    out_recv,
):
    f_local, p_local, width = x_hbm.shape
    f_own, count = whole.shape[:2]
    pt = p_local // n_tm
    pieces = PACK // pt
    piece = width // pieces
    n = n_tm * n_patch
    frames = f_local * n_tm
    i = lax.axis_index("tm")
    j = lax.axis_index("patch")
    me = j * n_tm + i

    barrier = pltpu.get_barrier_semaphore()

    def greet(k, carry):
        other = lax.rem(me + k, n)
        pl.semaphore_signal(
            barrier,
            inc=1,
            device_id=(lax.rem(other, n_tm), other // n_tm),
            device_id_type=MESH,
        )
        return carry

    lax.fori_loop(1, n, greet, 0)
    sources = (qkv_space_hbm, out_space_hbm, qkv_time_hbm, out_time_hbm, codebook_hbm)
    targets = (qkv_space, out_space, qkv_time, out_time, codebook)
    loads = [
        pltpu.make_async_copy(source, target, load_sem.at[k])
        for k, (source, target) in enumerate(zip(sources, targets))
    ]
    pl.semaphore_wait(barrier, n - 1)

    rows = pl.ds(pl.multiple_of(j * p_local, p_local), p_local)
    for f in range(f_own):
        for k in range(1, n_patch):
            to = lax.rem(j + k, n_patch)
            pltpu.make_async_remote_copy(
                src_ref=x_hbm.at[to * f_own + f],
                dst_ref=whole.at[f, rows],
                send_sem=in_send,
                recv_sem=in_recv.at[f],
                device_id=(i, to),
                device_id_type=MESH,
            ).start()
        pltpu.make_async_copy(x_hbm.at[j * f_own + f], whole.at[f, rows], in_recv.at[f]).start()
    for k in (4, 0, 1, 2, 3):
        loads[k].start()

    loads[4].wait()
    code_columns = jnp.transpose(codes_ref[...].astype(jnp.float32))
    code_ids = lax.broadcasted_iota(jnp.int32, (p_local, codebook.shape[0]), 1).astype(jnp.float32)
    for f in range(f_local):
        one_hot = jnp.where(code_columns[:, f : f + 1] == code_ids, 1.0, 0.0).astype(jnp.bfloat16)
        chosen[f] = jnp.dot(
            one_hot, codebook[...], preferred_element_type=jnp.float32
        ).astype(jnp.bfloat16)

    loads[0].wait()
    loads[1].wait()
    for f in range(f_own):
        pltpu.make_async_copy(whole.at[f], whole.at[f], in_recv.at[f]).wait()
        stream = attend(
            whole[f].astype(jnp.float32),
            gain_space[...],
            qkv_space,
            out_space,
            scale_space,
            None,
            normed_s,
            attn_s,
        )
        blocks = stream.reshape(n, pt, width)
        packed[f] = jnp.concatenate(
            [blocks[:, :, c * piece : (c + 1) * piece] for c in range(pieces)], 1
        ).astype(jnp.bfloat16)
        frame = i * f_local + j * f_own + f

        def send(k, carry):
            other = lax.rem(me + k, n)
            pltpu.make_async_remote_copy(
                src_ref=packed.at[f, other],
                dst_ref=arrived.at[frame],
                send_sem=mid_send,
                recv_sem=mid_recv,
                device_id=(lax.rem(other, n_tm), other // n_tm),
                device_id_type=MESH,
            ).start()
            return carry

        lax.fori_loop(1, n, send, 0)
        pltpu.make_async_copy(packed.at[f, me], arrived.at[frame], mid_recv).start()

    loads[2].wait()
    loads[3].wait()
    pltpu.make_async_copy(arrived, arrived, mid_recv).wait()
    for c in range(pieces):
        wide[:, :, c * piece : (c + 1) * piece] = arrived[:, c * pt : (c + 1) * pt, :].astype(
            jnp.float32
        )
    together = max(1, min(pt, LANES // frames))
    size = together * frames
    row = lax.broadcasted_iota(jnp.int32, (size, size), 0)
    column = lax.broadcasted_iota(jnp.int32, (size, size), 1)
    allowed = (row // frames == column // frames) & (row >= column)
    for first in range(0, pt, together):
        x = jnp.concatenate([wide[:, p, :] for p in range(first, first + together)], 0)
        result = attend(
            x, gain_time[...], qkv_time, out_time, scale_time, allowed, normed_t, attn_t
        )
        for p in range(together):
            wide[:, first + p, :] = result[p * frames : (p + 1) * frames]
    for k in range(n_tm):
        leaving[k] = (
            wide[k * f_local : (k + 1) * f_local].reshape(f_local * pt, width).astype(jnp.bfloat16)
        )

    def send_back(k, carry):
        to = lax.rem(i + k, n_tm)
        pltpu.make_async_remote_copy(
            src_ref=leaving.at[to],
            dst_ref=landed.at[i],
            send_sem=out_send,
            recv_sem=out_recv,
            device_id=(to, j),
            device_id_type=MESH,
        ).start()
        return carry

    lax.fori_loop(1, n_tm, send_back, 0)
    pltpu.make_async_copy(leaving.at[i], landed.at[i], out_recv).start()
    pltpu.make_async_copy(landed, landed, out_recv).wait()
    for first in range(0, n_tm, pieces):
        output = jnp.concatenate(
            [
                landed[first + k].astype(jnp.float32).reshape(f_local, pt, width)
                for k in range(pieces)
            ],
            1,
        )
        part = pl.ds(first * pt, PACK)
        encoded[:, part, :] = output.astype(jnp.bfloat16)
        commitment[:, part, :] = (output - chosen[:, part, :].astype(jnp.float32)).astype(
            jnp.bfloat16
        )

    sent = x_hbm.at[pl.ds(0, f_local - f_own)]
    pltpu.make_async_copy(sent, sent, in_send).wait()
    sent = packed.at[:, pl.ds(0, n - 1)]
    pltpu.make_async_copy(sent, sent, mid_send).wait()
    sent = leaving.at[pl.ds(0, n_tm - 1)]
    pltpu.make_async_copy(sent, sent, out_send).wait()


def solution(mesh):
    n_tm, n_patch = mesh.shape["tm"], mesh.shape["patch"]
    n = n_tm * n_patch

    def shards(x, codes, g_s, w_s, o_s, s_s, g_t, w_t, o_t, s_t, book):
        f_local, p_local, width = x.shape
        f_own, count = f_local // n_patch, p_local * n_patch
        frames, pt = f_local * n_tm, p_local // n_tm
        pieces = PACK // pt
        size = max(1, min(pt, LANES // frames)) * frames
        any_space = pl.BlockSpec(memory_space=pl.ANY)
        vmem = pl.BlockSpec(memory_space=pltpu.VMEM)
        smem = pl.BlockSpec(memory_space=pltpu.SMEM)
        bf16, f32 = jnp.bfloat16, jnp.float32
        return pl.pallas_call(
            functools.partial(kernel, n_tm, n_patch),
            out_shape=[jax.ShapeDtypeStruct(x.shape, bf16)] * 2,
            in_specs=[
                any_space,
                vmem,
                vmem,
                any_space,
                any_space,
                smem,
                vmem,
                any_space,
                any_space,
                smem,
                any_space,
            ],
            out_specs=[vmem, vmem],
            scratch_shapes=[
                pltpu.VMEM(w_s.shape, bf16),
                pltpu.VMEM(o_s.shape, bf16),
                pltpu.VMEM(w_t.shape, bf16),
                pltpu.VMEM(o_t.shape, bf16),
                pltpu.VMEM(book.shape, bf16),
                pltpu.VMEM((f_own, count, width), bf16),
                pltpu.VMEM((f_own, n, PACK, width // pieces), bf16),
                pltpu.VMEM((frames, PACK, width // pieces), bf16),
                pltpu.VMEM((frames, pt, width), f32),
                pltpu.VMEM((n_tm, f_local * pt, width), bf16),
                pltpu.VMEM((n_tm, f_local * pt, width), bf16),
                pltpu.VMEM(x.shape, bf16),
                pltpu.VMEM((count, width), bf16),
                pltpu.VMEM((count, width), bf16),
                pltpu.VMEM((size, width), bf16),
                pltpu.VMEM((size, width), bf16),
                pltpu.SemaphoreType.DMA((5,)),
                pltpu.SemaphoreType.DMA,
                pltpu.SemaphoreType.DMA((f_own,)),
                pltpu.SemaphoreType.DMA,
                pltpu.SemaphoreType.DMA,
                pltpu.SemaphoreType.DMA,
                pltpu.SemaphoreType.DMA,
            ],
            compiler_params=pltpu.CompilerParams(
                collective_id=0, has_side_effects=True, vmem_limit_bytes=56 * 1024 * 1024
            ),
            cost_estimate=pl.CostEstimate(
                flops=12_000_000_000, bytes_accessed=24_000_000, transcendentals=4_000_000
            ),
        )(
            x,
            codes,
            g_s.reshape(1, -1),
            w_s,
            o_s,
            s_s,
            g_t.reshape(1, -1),
            w_t,
            o_t,
            s_t,
            book,
        )

    return jax.shard_map(
        shards,
        mesh=mesh,
        in_specs=(P("tm", "patch", None), P("tm", "patch")) + (P(),) * 9,
        out_specs=(P("tm", "patch", None), P("tm", "patch", None)),
        check_vma=False,
    )
```

```python
import functools

import jax
import jax.numpy as jnp
from jax import lax
from jax.experimental import pallas as pl
from jax.experimental.pallas import tpu as pltpu
from jax.sharding import PartitionSpec as P

HD = 64
LANES = 256
PACK = 16
LOG2_E = 1.4426950408889634
MESH = pl.DeviceIdType.MESH


def lane_heads(rows):
    return lax.broadcasted_iota(jnp.int32, (rows, LANES), 1) // HD


def attend(x, gain, qkv_ref, out_ref, scale_ref, allowed, normed, attn):
    count, width = x.shape
    heads = LANES // HD
    square = jnp.mean(x * x, -1, keepdims=True)
    normed[...] = (x * lax.rsqrt(square + 1e-05) * gain).astype(jnp.bfloat16)
    lane_head = lane_heads(1)
    own_head = lax.broadcasted_iota(jnp.int32, (LANES, LANES), 0) // HD == lane_heads(LANES)
    head_mean = jnp.where(own_head, 1.0 / HD, 0.0).astype(jnp.bfloat16)
    rows_head = lax.broadcasted_iota(jnp.int32, (heads * count, LANES), 0) // count
    head_sum = jnp.where(rows_head == lane_heads(heads * count), 1.0, 0.0).astype(jnp.bfloat16)

    def unit(part):
        mean = jnp.dot(
            (part * part).astype(jnp.bfloat16), head_mean, preferred_element_type=jnp.float32
        )
        return part * lax.rsqrt(mean + 1e-06)

    def group(g, carry):
        def project(block):
            columns = pl.ds(pl.multiple_of(block * width + g * LANES, LANES), LANES)
            return jnp.dot(normed[...], qkv_ref[:, columns], preferred_element_type=jnp.float32)

        scale = jnp.zeros((1, LANES), jnp.float32)
        for h in range(heads):
            scale = jnp.where(lane_head == h, scale_ref[g * heads + h], scale)
        query = unit(project(0)) * (scale * (LOG2_E / HD))
        key = unit(project(1)).astype(jnp.bfloat16)
        value = project(2)
        stacked = jnp.concatenate(
            [jnp.where(lane_head == h, query, 0.0).astype(jnp.bfloat16) for h in range(heads)], 0
        )
        values = jnp.concatenate(
            [jnp.where(lane_head == h, value, 0.0).astype(jnp.bfloat16) for h in range(heads)], 0
        )
        scores = lax.dot_general(
            stacked, key, (((1,), (1,)), ((), ())), preferred_element_type=jnp.float32
        )
        weights = []
        for h in range(heads):
            weight = jnp.exp2(scores[h * count : (h + 1) * count])
            if allowed is not None:
                weight = jnp.where(allowed, weight, 0.0)
            weights.append(weight.astype(jnp.bfloat16))
        weight = jnp.concatenate(weights, 1)
        total = jnp.dot(weight, values, preferred_element_type=jnp.float32)
        denom = jnp.dot(weight, head_sum, preferred_element_type=jnp.float32)
        columns = pl.ds(pl.multiple_of(g * LANES, LANES), LANES)
        attn[:, columns] = (total / denom).astype(jnp.bfloat16)
        return carry

    lax.fori_loop(0, width // LANES, group, 0, unroll=2)
    return x + jnp.dot(attn[...], out_ref[...], preferred_element_type=jnp.float32)


def kernel(
    n_tm,
    n_patch,
    x_hbm,
    codes_ref,
    gain_space,
    qkv_space_hbm,
    out_space_hbm,
    scale_space,
    gain_time,
    qkv_time_hbm,
    out_time_hbm,
    scale_time,
    codebook_hbm,
    encoded,
    commitment,
    qkv_space,
    out_space,
    qkv_time,
    out_time,
    codebook,
    whole,
    packed,
    arrived,
    wide,
    leaving,
    landed,
    chosen,
    normed_s,
    attn_s,
    normed_t,
    attn_t,
    load_sem,
    in_send,
    in_recv,
    mid_send,
    mid_recv,
    out_send,
    out_recv,
):
    f_local, p_local, width = x_hbm.shape
    f_own, count = whole.shape[:2]
    halves, piece = arrived.shape[0], arrived.shape[3]
    pg = p_local // n_tm // halves
    pieces = PACK // pg
    n = n_tm * n_patch
    frames = f_local * n_tm
    i = lax.axis_index("tm")
    j = lax.axis_index("patch")
    me = j * n_tm + i

    barrier = pltpu.get_barrier_semaphore()

    def greet(k, carry):
        other = lax.rem(me + k, n)
        pl.semaphore_signal(
            barrier,
            inc=1,
            device_id=(lax.rem(other, n_tm), other // n_tm),
            device_id_type=MESH,
        )
        return carry

    lax.fori_loop(1, n, greet, 0)
    sources = (qkv_space_hbm, out_space_hbm, qkv_time_hbm, out_time_hbm, codebook_hbm)
    targets = (qkv_space, out_space, qkv_time, out_time, codebook)
    loads = [
        pltpu.make_async_copy(source, target, load_sem.at[k])
        for k, (source, target) in enumerate(zip(sources, targets))
    ]
    pl.semaphore_wait(barrier, n - 1)

    rows = pl.ds(pl.multiple_of(j * p_local, p_local), p_local)

    def share(f):
        for k in range(1, n_patch):
            to = lax.rem(j + k, n_patch)
            pltpu.make_async_remote_copy(
                src_ref=x_hbm.at[to * f_own + f],
                dst_ref=whole.at[f, rows],
                send_sem=in_send.at[f],
                recv_sem=in_recv.at[f],
                device_id=(i, to),
                device_id_type=MESH,
            ).start()
        pltpu.make_async_copy(x_hbm.at[j * f_own + f], whole.at[f, rows], in_recv.at[f]).start()

    def shared(f):
        sent = x_hbm.at[pl.ds(0, n_patch - 1)]
        pltpu.make_async_copy(sent, sent, in_send.at[f]).wait()

    share(0)
    for k in (4, 0, 1, 2, 3):
        loads[k].start()

    loads[4].wait()
    code_columns = jnp.transpose(codes_ref[...].astype(jnp.float32))
    code_ids = lax.broadcasted_iota(jnp.int32, (p_local, codebook.shape[0]), 1).astype(jnp.float32)
    for f in range(f_local):
        one_hot = jnp.where(code_columns[:, f : f + 1] == code_ids, 1.0, 0.0).astype(jnp.bfloat16)
        chosen[f] = jnp.dot(
            one_hot, codebook[...], preferred_element_type=jnp.float32
        ).astype(jnp.bfloat16)

    loads[0].wait()
    loads[1].wait()
    for f in range(1, f_own):
        shared(f - 1)
        share(f)
    for f in range(f_own):
        pltpu.make_async_copy(whole.at[f], whole.at[f], in_recv.at[f]).wait()
        stream = attend(
            whole[f].astype(jnp.float32),
            gain_space[...],
            qkv_space,
            out_space,
            scale_space,
            None,
            normed_s,
            attn_s,
        )
        blocks = stream.reshape(n * halves, pg, width)
        packed[f] = (
            jnp.concatenate([blocks[:, :, c * piece : (c + 1) * piece] for c in range(pieces)], 1)
            .astype(jnp.bfloat16)
            .reshape(packed.shape[1:])
        )
        frame = i * f_local + j * f_own + f
        last = f == f_own - 1

        def send(k, carry, half):
            other = lax.rem(me + k, n)
            to_i, to_j = lax.rem(other, n_tm), other // n_tm
            part = half if last else slice(None)
            pltpu.make_async_remote_copy(
                src_ref=packed.at[f, to_j, part, to_i],
                dst_ref=arrived.at[part, frame],
                send_sem=mid_send,
                recv_sem=mid_recv.at[half if last else halves],
                device_id=(to_i, to_j),
                device_id_type=MESH,
            ).start()
            return carry

        for half in range(halves if last else 1):
            part = half if last else slice(None)
            lax.fori_loop(1, n, functools.partial(send, half=half), 0)
            pltpu.make_async_copy(
                packed.at[f, j, part, i],
                arrived.at[part, frame],
                mid_recv.at[half if last else halves],
            ).start()

    loads[2].wait()
    loads[3].wait()
    row = lax.broadcasted_iota(jnp.int32, (LANES, LANES), 0)
    column = lax.broadcasted_iota(jnp.int32, (LANES, LANES), 1)
    allowed = (lax.rem(row, pg) == lax.rem(column, pg)) & (row >= column)
    if f_own > 1:
        early = arrived.at[:, pl.ds(0, (f_own - 1) * n)]
        pltpu.make_async_copy(early, early, mid_recv.at[halves]).wait()
    for half in range(halves):
        late = arrived.at[half, pl.ds(0, n)]
        pltpu.make_async_copy(late, late, mid_recv.at[half]).wait()
        for c in range(pieces):
            wide[:, c * piece : (c + 1) * piece] = (
                arrived[half, :, c * pg : (c + 1) * pg, :]
                .astype(jnp.float32)
                .reshape(LANES, piece)
            )
        result = attend(
            wide[...], gain_time[...], qkv_time, out_time, scale_time, allowed, normed_t, attn_t
        )
        leaving[half] = result.astype(jnp.bfloat16).reshape(leaving.shape[1:])

        def send_back(k, carry):
            to = lax.rem(i + k, n_tm)
            pltpu.make_async_remote_copy(
                src_ref=leaving.at[half, to],
                dst_ref=landed.at[half, i],
                send_sem=out_send,
                recv_sem=out_recv.at[half],
                device_id=(to, j),
                device_id_type=MESH,
            ).start()
            return carry

        lax.fori_loop(1, n_tm, send_back, 0)
        pltpu.make_async_copy(leaving.at[half, i], landed.at[half, i], out_recv.at[half]).start()

    for half in range(halves):
        pltpu.make_async_copy(landed.at[half], landed.at[half], out_recv.at[half]).wait()
        for first in range(0, n_tm, pieces):
            output = jnp.concatenate(
                [
                    landed[half, first + k].astype(jnp.float32).reshape(f_local, pg, width)
                    for k in range(pieces)
                ],
                1,
            )
            part = pl.ds(half * (p_local // halves) + first * pg, PACK)
            encoded[:, part, :] = output.astype(jnp.bfloat16)
            commitment[:, part, :] = (output - chosen[:, part, :].astype(jnp.float32)).astype(
                jnp.bfloat16
            )

    shared(f_own - 1)
    for f in range(f_own):
        sent = packed.at[f, pl.ds(0, n_patch - 1)]
        pltpu.make_async_copy(sent, sent, mid_send).wait()
        sent = packed.at[f, 0, :, pl.ds(0, n_tm - 1)]
        pltpu.make_async_copy(sent, sent, mid_send).wait()
    sent = leaving.at[:, pl.ds(0, n_tm - 1)]
    pltpu.make_async_copy(sent, sent, out_send).wait()


def solution(mesh):
    n_tm, n_patch = mesh.shape["tm"], mesh.shape["patch"]
    n = n_tm * n_patch

    def shards(x, codes, g_s, w_s, o_s, s_s, g_t, w_t, o_t, s_t, book):
        f_local, p_local, width = x.shape
        f_own, count = f_local // n_patch, p_local * n_patch
        frames = f_local * n_tm
        pg = max(1, LANES // frames)
        halves = p_local // n_tm // pg
        piece = width * pg // PACK
        any_space = pl.BlockSpec(memory_space=pl.ANY)
        vmem = pl.BlockSpec(memory_space=pltpu.VMEM)
        smem = pl.BlockSpec(memory_space=pltpu.SMEM)
        bf16, f32 = jnp.bfloat16, jnp.float32
        return pl.pallas_call(
            functools.partial(kernel, n_tm, n_patch),
            out_shape=[jax.ShapeDtypeStruct(x.shape, bf16)] * 2,
            in_specs=[
                any_space,
                vmem,
                vmem,
                any_space,
                any_space,
                smem,
                vmem,
                any_space,
                any_space,
                smem,
                any_space,
            ],
            out_specs=[vmem, vmem],
            scratch_shapes=[
                pltpu.VMEM(w_s.shape, bf16),
                pltpu.VMEM(o_s.shape, bf16),
                pltpu.VMEM(w_t.shape, bf16),
                pltpu.VMEM(o_t.shape, bf16),
                pltpu.VMEM(book.shape, bf16),
                pltpu.VMEM((f_own, count, width), bf16),
                pltpu.VMEM((f_own, n_patch, halves, n_tm, PACK, piece), bf16),
                pltpu.VMEM((halves, frames, PACK, piece), bf16),
                pltpu.VMEM((LANES, width), f32),
                pltpu.VMEM((halves, n_tm, f_local * pg, width), bf16),
                pltpu.VMEM((halves, n_tm, f_local * pg, width), bf16),
                pltpu.VMEM(x.shape, bf16),
                pltpu.VMEM((count, width), bf16),
                pltpu.VMEM((count, width), bf16),
                pltpu.VMEM((LANES, width), bf16),
                pltpu.VMEM((LANES, width), bf16),
                pltpu.SemaphoreType.DMA((5,)),
                pltpu.SemaphoreType.DMA((f_own,)),
                pltpu.SemaphoreType.DMA((f_own,)),
                pltpu.SemaphoreType.DMA,
                pltpu.SemaphoreType.DMA((halves + 1,)),
                pltpu.SemaphoreType.DMA,
                pltpu.SemaphoreType.DMA((halves,)),
            ],
            compiler_params=pltpu.CompilerParams(
                collective_id=0, has_side_effects=True, vmem_limit_bytes=56 * 1024 * 1024
            ),
            cost_estimate=pl.CostEstimate(
                flops=12_000_000_000, bytes_accessed=24_000_000, transcendentals=4_000_000
            ),
        )(
            x,
            codes,
            g_s.reshape(1, -1),
            w_s,
            o_s,
            s_s,
            g_t.reshape(1, -1),
            w_t,
            o_t,
            s_t,
            book,
        )

    return jax.shard_map(
        shards,
        mesh=mesh,
        in_specs=(P("tm", "patch", None), P("tm", "patch")) + (P(),) * 9,
        out_specs=(P("tm", "patch", None), P("tm", "patch", None)),
        check_vma=False,
    )
```

```python
import functools

import jax
import jax.numpy as jnp
from jax import lax
from jax.experimental import pallas as pl
from jax.experimental.pallas import tpu as pltpu
from jax.sharding import PartitionSpec as P

HD = 64
LANES = 256
PACK = 16
LOG2_E = 1.4426950408889634
MESH = pl.DeviceIdType.MESH


def fill_masks(head_mean, head_sum, head_rows, allowed, pg):
    heads = LANES // HD
    row = lax.broadcasted_iota(jnp.int32, (LANES, LANES), 0)
    column = lax.broadcasted_iota(jnp.int32, (LANES, LANES), 1)
    head_mean[...] = jnp.where(row // HD == column // HD, 1.0 / HD, 0.0).astype(jnp.bfloat16)
    count = head_sum.shape[0] // heads
    wide_column = lax.broadcasted_iota(jnp.int32, (count, LANES), 1)
    few_columns = lax.broadcasted_iota(jnp.int32, (PACK, LANES), 1)
    for h in range(heads):
        head_sum[h * count : (h + 1) * count] = jnp.where(
            wide_column // HD == h, 1.0, 0.0
        ).astype(jnp.bfloat16)
        head_rows[h] = jnp.where(few_columns // HD == h, 1.0, 0.0).astype(jnp.bfloat16)
    allowed[...] = jnp.where(
        (lax.rem(row, pg) == lax.rem(column, pg)) & (row >= column), 1.0, 0.0
    ).astype(jnp.bfloat16)


def attend(x, gain, qkv_ref, out_ref, scale_ref, masks, allowed, normed, attn):
    head_mean, head_sum, head_rows = masks
    count, width = x.shape
    heads = LANES // HD
    square = jnp.mean(x * x, -1, keepdims=True)
    normed[...] = (x * lax.rsqrt(square + 1e-05) * gain).astype(jnp.bfloat16)
    lane_head = lax.broadcasted_iota(jnp.int32, (1, LANES), 1) // HD
    step = head_sum.shape[0] // heads

    def unit(part):
        mean = jnp.dot(
            (part * part).astype(jnp.bfloat16), head_mean[...], preferred_element_type=jnp.float32
        )
        return part * lax.rsqrt(mean + 1e-06)

    def by_head(part):
        return jnp.concatenate([part * head_rows[h][:1] for h in range(heads)], 0)

    def prepare(g):
        def project(block):
            first = block * width + g * LANES
            return jnp.dot(
                normed[...], qkv_ref[:, first : first + LANES], preferred_element_type=jnp.float32
            )

        scale = jnp.zeros((1, LANES), jnp.float32)
        for h in range(heads):
            scale = jnp.where(lane_head == h, scale_ref[g * heads + h], scale)
        query = (unit(project(0)) * (scale * (LOG2_E / HD))).astype(jnp.bfloat16)
        key = unit(project(1)).astype(jnp.bfloat16)
        value = project(2).astype(jnp.bfloat16)
        return by_head(query), key, by_head(value)

    ready = prepare(0)
    for g in range(width // LANES):
        stacked, key, values = ready
        scores = lax.dot_general(
            stacked, key, (((1,), (1,)), ((), ())), preferred_element_type=jnp.float32
        )
        if (g + 1) * LANES < width:
            ready = prepare(g + 1)
        weights = []
        for h in range(heads):
            weight = jnp.exp2(scores[h * count : (h + 1) * count]).astype(jnp.bfloat16)
            weights.append(weight if allowed is None else weight * allowed[...])
        weight = jnp.concatenate(weights, 1)
        total = jnp.dot(weight, values, preferred_element_type=jnp.float32)
        if step == count:
            sums = head_sum[...]
        else:
            sums = jnp.concatenate(
                [head_sum[h * step : h * step + count] for h in range(heads)], 0
            )
        denom = jnp.dot(weight, sums, preferred_element_type=jnp.float32)
        attn[:, g * LANES : (g + 1) * LANES] = (total / denom).astype(jnp.bfloat16)
    return x + jnp.dot(attn[...], out_ref[...], preferred_element_type=jnp.float32)


def kernel(
    n_tm,
    n_patch,
    x_hbm,
    codes_ref,
    gain_space,
    qkv_space_hbm,
    out_space_hbm,
    scale_space,
    gain_time,
    qkv_time_hbm,
    out_time_hbm,
    scale_time,
    codebook_hbm,
    encoded,
    commitment,
    qkv_space,
    out_space,
    qkv_time,
    out_time,
    codebook,
    whole,
    packed,
    arrived,
    wide,
    leaving,
    landed,
    chosen,
    normed_s,
    attn_s,
    normed_t,
    attn_t,
    head_mean,
    head_sum,
    head_rows,
    allowed,
    load_sem,
    in_send,
    in_recv,
    mid_send,
    mid_recv,
    out_send,
    out_recv,
):
    f_local, p_local, width = x_hbm.shape
    f_own, count = whole.shape[:2]
    halves, piece = arrived.shape[0], arrived.shape[3]
    pg = p_local // n_tm // halves
    pieces = PACK // pg
    n = n_tm * n_patch
    frames = f_local * n_tm
    i = lax.axis_index("tm")
    j = lax.axis_index("patch")
    me = j * n_tm + i

    barrier = pltpu.get_barrier_semaphore()

    def greet(k, carry):
        other = lax.rem(me + k, n)
        pl.semaphore_signal(
            barrier,
            inc=1,
            device_id=(lax.rem(other, n_tm), other // n_tm),
            device_id_type=MESH,
        )
        return carry

    lax.fori_loop(1, n, greet, 0)
    sources = (qkv_space_hbm, out_space_hbm, qkv_time_hbm, out_time_hbm, codebook_hbm)
    targets = (qkv_space, out_space, qkv_time, out_time, codebook)
    loads = [
        pltpu.make_async_copy(source, target, load_sem.at[k])
        for k, (source, target) in enumerate(zip(sources, targets))
    ]
    pl.semaphore_wait(barrier, n - 1)

    rows = pl.ds(pl.multiple_of(j * p_local, p_local), p_local)

    def share(f):
        for k in range(1, n_patch):
            to = lax.rem(j + k, n_patch)
            pltpu.make_async_remote_copy(
                src_ref=x_hbm.at[to * f_own + f],
                dst_ref=whole.at[f, rows],
                send_sem=in_send.at[f],
                recv_sem=in_recv.at[f],
                device_id=(i, to),
                device_id_type=MESH,
            ).start()
        pltpu.make_async_copy(x_hbm.at[j * f_own + f], whole.at[f, rows], in_recv.at[f]).start()

    def shared(f):
        sent = x_hbm.at[pl.ds(0, n_patch - 1)]
        pltpu.make_async_copy(sent, sent, in_send.at[f]).wait()

    share(0)
    for k in (4, 0, 1, 2, 3):
        loads[k].start()

    fill_masks(head_mean, head_sum, head_rows, allowed, pg)
    masks = (head_mean, head_sum, head_rows)
    loads[4].wait()
    code_columns = jnp.transpose(codes_ref[...].astype(jnp.float32))
    code_ids = lax.broadcasted_iota(jnp.int32, (p_local, codebook.shape[0]), 1).astype(jnp.float32)
    for f in range(f_local):
        one_hot = jnp.where(code_columns[:, f : f + 1] == code_ids, 1.0, 0.0).astype(jnp.bfloat16)
        chosen[f] = jnp.dot(
            one_hot, codebook[...], preferred_element_type=jnp.float32
        ).astype(jnp.bfloat16)

    loads[0].wait()
    loads[1].wait()
    for f in range(1, f_own):
        shared(f - 1)
        share(f)
    for f in range(f_own):
        pltpu.make_async_copy(whole.at[f], whole.at[f], in_recv.at[f]).wait()
        stream = attend(
            whole[f].astype(jnp.float32),
            gain_space[...],
            qkv_space,
            out_space,
            scale_space,
            masks,
            None,
            normed_s,
            attn_s,
        )
        blocks = stream.reshape(n * halves, pg, width)
        packed[f] = (
            jnp.concatenate([blocks[:, :, c * piece : (c + 1) * piece] for c in range(pieces)], 1)
            .astype(jnp.bfloat16)
            .reshape(packed.shape[1:])
        )
        frame = i * f_local + j * f_own + f
        last = f == f_own - 1

        def send(k, carry, half):
            other = lax.rem(me + k, n)
            to_i, to_j = lax.rem(other, n_tm), other // n_tm
            part = half if last else slice(None)
            pltpu.make_async_remote_copy(
                src_ref=packed.at[f, to_j, part, to_i],
                dst_ref=arrived.at[part, frame],
                send_sem=mid_send,
                recv_sem=mid_recv.at[half if last else halves],
                device_id=(to_i, to_j),
                device_id_type=MESH,
            ).start()
            return carry

        for half in range(halves if last else 1):
            part = half if last else slice(None)
            lax.fori_loop(1, n, functools.partial(send, half=half), 0)
            pltpu.make_async_copy(
                packed.at[f, j, part, i],
                arrived.at[part, frame],
                mid_recv.at[half if last else halves],
            ).start()

    loads[2].wait()
    loads[3].wait()
    if f_own > 1:
        early = arrived.at[:, pl.ds(0, (f_own - 1) * n)]
        pltpu.make_async_copy(early, early, mid_recv.at[halves]).wait()
    for half in range(halves):
        late = arrived.at[half, pl.ds(0, n)]
        pltpu.make_async_copy(late, late, mid_recv.at[half]).wait()
        for c in range(pieces):
            wide[:, c * piece : (c + 1) * piece] = (
                arrived[half, :, c * pg : (c + 1) * pg, :]
                .astype(jnp.float32)
                .reshape(LANES, piece)
            )
        result = attend(
            wide[...],
            gain_time[...],
            qkv_time,
            out_time,
            scale_time,
            masks,
            allowed,
            normed_t,
            attn_t,

        )
        leaving[half] = result.astype(jnp.bfloat16).reshape(leaving.shape[1:])

        def send_back(k, carry):
            to = lax.rem(i + k, n_tm)
            pltpu.make_async_remote_copy(
                src_ref=leaving.at[half, to],
                dst_ref=landed.at[half, i],
                send_sem=out_send,
                recv_sem=out_recv.at[half],
                device_id=(to, j),
                device_id_type=MESH,
            ).start()
            return carry

        lax.fori_loop(1, n_tm, send_back, 0)
        pltpu.make_async_copy(leaving.at[half, i], landed.at[half, i], out_recv.at[half]).start()

    for half in range(halves):
        pltpu.make_async_copy(landed.at[half], landed.at[half], out_recv.at[half]).wait()
        for first in range(0, n_tm, pieces):
            output = jnp.concatenate(
                [
                    landed[half, first + k].astype(jnp.float32).reshape(f_local, pg, width)
                    for k in range(pieces)
                ],
                1,
            )
            part = pl.ds(half * (p_local // halves) + first * pg, PACK)
            encoded[:, part, :] = output.astype(jnp.bfloat16)
            commitment[:, part, :] = (output - chosen[:, part, :].astype(jnp.float32)).astype(
                jnp.bfloat16
            )

    shared(f_own - 1)
    for f in range(f_own):
        sent = packed.at[f, pl.ds(0, n_patch - 1)]
        pltpu.make_async_copy(sent, sent, mid_send).wait()
        sent = packed.at[f, 0, :, pl.ds(0, n_tm - 1)]
        pltpu.make_async_copy(sent, sent, mid_send).wait()
    sent = leaving.at[:, pl.ds(0, n_tm - 1)]
    pltpu.make_async_copy(sent, sent, out_send).wait()


def solution(mesh):
    n_tm, n_patch = mesh.shape["tm"], mesh.shape["patch"]
    n = n_tm * n_patch

    def shards(x, codes, g_s, w_s, o_s, s_s, g_t, w_t, o_t, s_t, book):
        f_local, p_local, width = x.shape
        f_own, count = f_local // n_patch, p_local * n_patch
        frames = f_local * n_tm
        pg = max(1, LANES // frames)
        halves = p_local // n_tm // pg
        piece = width * pg // PACK
        any_space = pl.BlockSpec(memory_space=pl.ANY)
        vmem = pl.BlockSpec(memory_space=pltpu.VMEM)
        smem = pl.BlockSpec(memory_space=pltpu.SMEM)
        bf16, f32 = jnp.bfloat16, jnp.float32
        return pl.pallas_call(
            functools.partial(kernel, n_tm, n_patch),
            out_shape=[jax.ShapeDtypeStruct(x.shape, bf16)] * 2,
            in_specs=[
                any_space,
                vmem,
                vmem,
                any_space,
                any_space,
                smem,
                vmem,
                any_space,
                any_space,
                smem,
                any_space,
            ],
            out_specs=[vmem, vmem],
            scratch_shapes=[
                pltpu.VMEM(w_s.shape, bf16),
                pltpu.VMEM(o_s.shape, bf16),
                pltpu.VMEM(w_t.shape, bf16),
                pltpu.VMEM(o_t.shape, bf16),
                pltpu.VMEM(book.shape, bf16),
                pltpu.VMEM((f_own, count, width), bf16),
                pltpu.VMEM((f_own, n_patch, halves, n_tm, PACK, piece), bf16),
                pltpu.VMEM((halves, frames, PACK, piece), bf16),
                pltpu.VMEM((LANES, width), f32),
                pltpu.VMEM((halves, n_tm, f_local * pg, width), bf16),
                pltpu.VMEM((halves, n_tm, f_local * pg, width), bf16),
                pltpu.VMEM(x.shape, bf16),
                pltpu.VMEM((count, width), bf16),
                pltpu.VMEM((count, width), bf16),
                pltpu.VMEM((LANES, width), bf16),
                pltpu.VMEM((LANES, width), bf16),
                pltpu.VMEM((LANES, LANES), bf16),
                pltpu.VMEM((LANES // HD * max(count, LANES), LANES), bf16),
                pltpu.VMEM((LANES // HD, PACK, LANES), bf16),
                pltpu.VMEM((LANES, LANES), bf16),
                pltpu.SemaphoreType.DMA((5,)),
                pltpu.SemaphoreType.DMA((f_own,)),
                pltpu.SemaphoreType.DMA((f_own,)),
                pltpu.SemaphoreType.DMA,
                pltpu.SemaphoreType.DMA((halves + 1,)),
                pltpu.SemaphoreType.DMA,
                pltpu.SemaphoreType.DMA((halves,)),
            ],
            compiler_params=pltpu.CompilerParams(
                collective_id=0, has_side_effects=True, vmem_limit_bytes=56 * 1024 * 1024
            ),
            cost_estimate=pl.CostEstimate(
                flops=12_000_000_000, bytes_accessed=24_000_000, transcendentals=4_000_000
            ),
        )(
            x,
            codes,
            g_s.reshape(1, -1),
            w_s,
            o_s,
            s_s,
            g_t.reshape(1, -1),
            w_t,
            o_t,
            s_t,
            book,
        )

    return jax.shard_map(
        shards,
        mesh=mesh,
        in_specs=(P("tm", "patch", None), P("tm", "patch")) + (P(),) * 9,
        out_specs=(P("tm", "patch", None), P("tm", "patch", None)),
        check_vma=False,
    )
```

```python
import functools

import jax
import jax.numpy as jnp
from jax import lax
from jax.experimental import pallas as pl
from jax.experimental.pallas import tpu as pltpu
from jax.sharding import PartitionSpec as P

HD = 64
LANES = 256
PACK = 16
LOG2_E = 1.4426950408889634
MESH = pl.DeviceIdType.MESH


def fill_masks(head_mean, head_sum, head_rows, allowed, pg):
    heads = LANES // HD
    row = lax.broadcasted_iota(jnp.int32, (LANES, LANES), 0)
    column = lax.broadcasted_iota(jnp.int32, (LANES, LANES), 1)
    head_mean[...] = jnp.where(row // HD == column // HD, 1.0 / HD, 0.0).astype(jnp.bfloat16)
    few_columns = lax.broadcasted_iota(jnp.int32, (PACK, LANES), 1)
    for h in range(heads):
        across = (h + heads // 2) % heads
        head_sum[h] = jnp.where(few_columns // HD == across, 1.0, 0.0).astype(jnp.bfloat16)
        head_rows[h] = jnp.where(few_columns // HD == h, 1.0, 0.0).astype(jnp.bfloat16)
    allowed[...] = jnp.where(
        (lax.rem(row, pg) == lax.rem(column, pg)) & (row >= column), 1.0, 0.0
    ).astype(jnp.bfloat16)


def attend(x, gain, qkv_ref, out_ref, scale_ref, masks, allowed, normed, attn):
    head_mean, head_sum, head_rows = masks
    count, width = x.shape
    heads = LANES // HD
    square = jnp.mean(x * x, -1, keepdims=True)
    normed[...] = (x * lax.rsqrt(square + 1e-05) * gain).astype(jnp.bfloat16)
    lane_head = lax.broadcasted_iota(jnp.int32, (1, LANES), 1) // HD
    pair, split = heads // 2, LANES // 2

    def unit(part):
        mean = jnp.dot(
            (part * part).astype(jnp.bfloat16), head_mean[...], preferred_element_type=jnp.float32
        )
        return part * lax.rsqrt(mean + 1e-06)

    def by_head(part):
        return jnp.concatenate([part * head_rows[h][:1] for h in range(heads)], 0)

    def prepare(g):
        def project(block):
            first = block * width + g * LANES
            return jnp.dot(
                normed[...], qkv_ref[:, first : first + LANES], preferred_element_type=jnp.float32
            )

        scale = jnp.zeros((1, LANES), jnp.float32)
        for h in range(heads):
            scale = jnp.where(lane_head == h, scale_ref[g * heads + h], scale)
        query = (unit(project(0)) * (scale * (LOG2_E / HD))).astype(jnp.bfloat16)
        key = unit(project(1)).astype(jnp.bfloat16)
        value = project(2).astype(jnp.bfloat16)
        values = [
            jnp.concatenate(
                [value * head_rows[h][:1] + head_sum[h][:1] for h in range(first, first + pair)], 0
            )
            for first in range(0, heads, pair)
        ]
        return by_head(query), key, values

    ready = prepare(0)
    for g in range(width // LANES):
        stacked, key, values = ready
        scores = lax.dot_general(
            stacked, key, (((1,), (1,)), ((), ())), preferred_element_type=jnp.float32
        )
        if (g + 1) * LANES < width:
            ready = prepare(g + 1)
        weights = []
        for h in range(heads):
            weight = jnp.exp2(scores[h * count : (h + 1) * count]).astype(jnp.bfloat16)
            weights.append(weight if allowed is None else weight * allowed[...])
        low, high = (
            jnp.dot(
                jnp.concatenate(weights[first : first + pair], 1),
                values[first // pair],
                preferred_element_type=jnp.float32,
            )
            for first in (0, pair)
        )
        columns = g * LANES
        attn[:, columns : columns + split] = (low[:, :split] / low[:, split:]).astype(jnp.bfloat16)
        attn[:, columns + split : columns + LANES] = (high[:, split:] / high[:, :split]).astype(
            jnp.bfloat16
        )
    return x + jnp.dot(attn[...], out_ref[...], preferred_element_type=jnp.float32)


def kernel(
    n_tm,
    n_patch,
    x_hbm,
    codes_ref,
    gain_space,
    qkv_space_hbm,
    out_space_hbm,
    scale_space,
    gain_time,
    qkv_time_hbm,
    out_time_hbm,
    scale_time,
    codebook_hbm,
    encoded,
    chosen_out,
    qkv_space,
    out_space,
    qkv_time,
    out_time,
    codebook,
    whole,
    packed,
    arrived,
    wide,
    leaving,
    landed,
    chosen,
    normed_s,
    attn_s,
    normed_t,
    attn_t,
    head_mean,
    head_sum,
    head_rows,
    allowed,
    load_sem,
    in_send,
    in_recv,
    mid_send,
    mid_recv,
    out_send,
    out_recv,
):
    f_local, p_local, width = x_hbm.shape
    f_own, count = whole.shape[:2]
    halves, piece = arrived.shape[0], arrived.shape[3]
    pg = p_local // n_tm // halves
    pieces = PACK // pg
    n = n_tm * n_patch
    frames = f_local * n_tm
    i = lax.axis_index("tm")
    j = lax.axis_index("patch")
    me = j * n_tm + i

    barrier = pltpu.get_barrier_semaphore()

    def greet(k, carry):
        other = lax.rem(me + k, n)
        pl.semaphore_signal(
            barrier,
            inc=1,
            device_id=(lax.rem(other, n_tm), other // n_tm),
            device_id_type=MESH,
        )
        return carry

    lax.fori_loop(1, n, greet, 0)
    sources = (qkv_space_hbm, out_space_hbm, qkv_time_hbm, out_time_hbm, codebook_hbm)
    targets = (qkv_space, out_space, qkv_time, out_time, codebook)
    loads = [
        pltpu.make_async_copy(source, target, load_sem.at[k])
        for k, (source, target) in enumerate(zip(sources, targets))
    ]
    pl.semaphore_wait(barrier, n - 1)

    rows = pl.ds(pl.multiple_of(j * p_local, p_local), p_local)

    def share(f):
        for k in range(1, n_patch):
            to = lax.rem(j + k, n_patch)
            pltpu.make_async_remote_copy(
                src_ref=x_hbm.at[to * f_own + f],
                dst_ref=whole.at[f, rows],
                send_sem=in_send.at[f],
                recv_sem=in_recv.at[f],
                device_id=(i, to),
                device_id_type=MESH,
            ).start()
        pltpu.make_async_copy(x_hbm.at[j * f_own + f], whole.at[f, rows], in_recv.at[f]).start()

    def shared(f):
        sent = x_hbm.at[pl.ds(0, n_patch - 1)]
        pltpu.make_async_copy(sent, sent, in_send.at[f]).wait()

    share(0)
    for k in (4, 0, 1, 2, 3):
        loads[k].start()

    fill_masks(head_mean, head_sum, head_rows, allowed, pg)
    masks = (head_mean, head_sum, head_rows)
    loads[4].wait()
    code_columns = jnp.transpose(codes_ref[...].astype(jnp.float32))
    code_ids = lax.broadcasted_iota(jnp.int32, (p_local, codebook.shape[0]), 1).astype(jnp.float32)
    for f in range(f_local):
        one_hot = jnp.where(code_columns[:, f : f + 1] == code_ids, 1.0, 0.0).astype(jnp.bfloat16)
        chosen[f] = jnp.dot(
            one_hot, codebook[...], preferred_element_type=jnp.float32
        ).astype(jnp.bfloat16)

    keep = pltpu.make_async_copy(chosen, chosen_out, load_sem.at[5])
    keep.start()
    loads[0].wait()
    loads[1].wait()
    for f in range(1, f_own):
        shared(f - 1)
        share(f)
    for f in range(f_own):
        pltpu.make_async_copy(whole.at[f], whole.at[f], in_recv.at[f]).wait()
        stream = attend(
            whole[f].astype(jnp.float32),
            gain_space[...],
            qkv_space,
            out_space,
            scale_space,
            masks,
            None,
            normed_s,
            attn_s,
        )
        blocks = stream.reshape(n * halves, pg, width)
        packed[f] = (
            jnp.concatenate([blocks[:, :, c * piece : (c + 1) * piece] for c in range(pieces)], 1)
            .astype(jnp.bfloat16)
            .reshape(packed.shape[1:])
        )
        frame = i * f_local + j * f_own + f
        last = f == f_own - 1

        def send(k, carry, half):
            other = lax.rem(me + 1 + lax.rem(k + n_tm - 2, n - 1), n)
            to_i, to_j = lax.rem(other, n_tm), other // n_tm
            part = half if last else slice(None)
            pltpu.make_async_remote_copy(
                src_ref=packed.at[f, to_j, part, to_i],
                dst_ref=arrived.at[part, frame],
                send_sem=mid_send,
                recv_sem=mid_recv.at[half if last else halves],
                device_id=(to_i, to_j),
                device_id_type=MESH,
            ).start()
            return carry

        for half in range(halves if last else 1):
            part = half if last else slice(None)
            lax.fori_loop(1, n, functools.partial(send, half=half), 0)
            pltpu.make_async_copy(
                packed.at[f, j, part, i],
                arrived.at[part, frame],
                mid_recv.at[half if last else halves],
            ).start()

    loads[2].wait()
    loads[3].wait()
    if f_own > 1:
        early = arrived.at[:, pl.ds(0, (f_own - 1) * n)]
        pltpu.make_async_copy(early, early, mid_recv.at[halves]).wait()
    for half in range(halves):
        late = arrived.at[half, pl.ds(0, n)]
        pltpu.make_async_copy(late, late, mid_recv.at[half]).wait()
        for c in range(pieces):
            wide[:, c * piece : (c + 1) * piece] = (
                arrived[half, :, c * pg : (c + 1) * pg, :]
                .astype(jnp.float32)
                .reshape(LANES, piece)
            )
        result = attend(
            wide[...],
            gain_time[...],
            qkv_time,
            out_time,
            scale_time,
            masks,
            allowed,
            normed_t,
            attn_t,

        )
        leaving[half] = result.astype(jnp.bfloat16).reshape(leaving.shape[1:])

        def send_back(k, carry):
            to = lax.rem(i + k, n_tm)
            pltpu.make_async_remote_copy(
                src_ref=leaving.at[half, to],
                dst_ref=landed.at[half, i],
                send_sem=out_send,
                recv_sem=out_recv.at[half],
                device_id=(to, j),
                device_id_type=MESH,
            ).start()
            return carry

        lax.fori_loop(1, n_tm, send_back, 0)
        pltpu.make_async_copy(leaving.at[half, i], landed.at[half, i], out_recv.at[half]).start()

    for half in range(halves):
        pltpu.make_async_copy(landed.at[half], landed.at[half], out_recv.at[half]).wait()
        for first in range(0, n_tm, pieces):
            output = jnp.concatenate(
                [
                    landed[half, first + k].astype(jnp.float32).reshape(f_local, pg, width)
                    for k in range(pieces)
                ],
                1,
            )
            part = pl.ds(half * (p_local // halves) + first * pg, PACK)
            encoded[:, part, :] = output.astype(jnp.bfloat16)

    keep.wait()
    shared(f_own - 1)
    for f in range(f_own):
        sent = packed.at[f, pl.ds(0, n_patch - 1)]
        pltpu.make_async_copy(sent, sent, mid_send).wait()
        sent = packed.at[f, 0, :, pl.ds(0, n_tm - 1)]
        pltpu.make_async_copy(sent, sent, mid_send).wait()
    sent = leaving.at[:, pl.ds(0, n_tm - 1)]
    pltpu.make_async_copy(sent, sent, out_send).wait()


def finish(output, rows, encoded, commitment):
    encoded[...] = output[...]
    commitment[...] = (
        output[...].astype(jnp.float32) - rows[...].astype(jnp.float32)
    ).astype(jnp.bfloat16)


def solution(mesh):
    n_tm, n_patch = mesh.shape["tm"], mesh.shape["patch"]
    n = n_tm * n_patch

    def shards(x, codes, g_s, w_s, o_s, s_s, g_t, w_t, o_t, s_t, book):
        f_local, p_local, width = x.shape
        f_own, count = f_local // n_patch, p_local * n_patch
        frames = f_local * n_tm
        pg = max(1, LANES // frames)
        halves = p_local // n_tm // pg
        piece = width * pg // PACK
        any_space = pl.BlockSpec(memory_space=pl.ANY)
        vmem = pl.BlockSpec(memory_space=pltpu.VMEM)
        smem = pl.BlockSpec(memory_space=pltpu.SMEM)
        bf16, f32 = jnp.bfloat16, jnp.float32
        output, rows = pl.pallas_call(
            functools.partial(kernel, n_tm, n_patch),
            out_shape=[jax.ShapeDtypeStruct(x.shape, bf16)] * 2,
            in_specs=[
                any_space,
                vmem,
                vmem,
                any_space,
                any_space,
                smem,
                vmem,
                any_space,
                any_space,
                smem,
                any_space,
            ],
            out_specs=[vmem, any_space],
            scratch_shapes=[
                pltpu.VMEM(w_s.shape, bf16),
                pltpu.VMEM(o_s.shape, bf16),
                pltpu.VMEM(w_t.shape, bf16),
                pltpu.VMEM(o_t.shape, bf16),
                pltpu.VMEM(book.shape, bf16),
                pltpu.VMEM((f_own, count, width), bf16),
                pltpu.VMEM((f_own, n_patch, halves, n_tm, PACK, piece), bf16),
                pltpu.VMEM((halves, frames, PACK, piece), bf16),
                pltpu.VMEM((LANES, width), f32),
                pltpu.VMEM((halves, n_tm, f_local * pg, width), bf16),
                pltpu.VMEM((halves, n_tm, f_local * pg, width), bf16),
                pltpu.VMEM(x.shape, bf16),
                pltpu.VMEM((count, width), bf16),
                pltpu.VMEM((count, width), bf16),
                pltpu.VMEM((LANES, width), bf16),
                pltpu.VMEM((LANES, width), bf16),
                pltpu.VMEM((LANES, LANES), bf16),
                pltpu.VMEM((LANES // HD, PACK, LANES), bf16),
                pltpu.VMEM((LANES // HD, PACK, LANES), bf16),
                pltpu.VMEM((LANES, LANES), bf16),
                pltpu.SemaphoreType.DMA((6,)),
                pltpu.SemaphoreType.DMA((f_own,)),
                pltpu.SemaphoreType.DMA((f_own,)),
                pltpu.SemaphoreType.DMA,
                pltpu.SemaphoreType.DMA((halves + 1,)),
                pltpu.SemaphoreType.DMA,
                pltpu.SemaphoreType.DMA((halves,)),
            ],
            compiler_params=pltpu.CompilerParams(
                collective_id=0, has_side_effects=True, vmem_limit_bytes=56 * 1024 * 1024
            ),
            cost_estimate=pl.CostEstimate(
                flops=12_000_000_000, bytes_accessed=24_000_000, transcendentals=4_000_000
            ),
        )(
            x,
            codes,
            g_s.reshape(1, -1),
            w_s,
            o_s,
            s_s,
            g_t.reshape(1, -1),
            w_t,
            o_t,
            s_t,
            book,
        )
        block = pl.BlockSpec((max(1, f_local // 4), p_local, width), lambda f: (f, 0, 0))
        return pl.pallas_call(
            finish,
            grid=(f_local // max(1, f_local // 4),),
            out_shape=[jax.ShapeDtypeStruct(x.shape, bf16)] * 2,
            in_specs=[block, block],
            out_specs=[block, block],
            compiler_params=pltpu.CompilerParams(vmem_limit_bytes=60 * 1024 * 1024),
        )(output, rows)

    return jax.shard_map(
        shards,
        mesh=mesh,
        in_specs=(P("tm", "patch", None), P("tm", "patch")) + (P(),) * 9,
        out_specs=(P("tm", "patch", None), P("tm", "patch", None)),
        check_vma=False,
    )
```

```python
import functools

import jax
import jax.numpy as jnp
from jax import lax
from jax.experimental import pallas as pl
from jax.experimental.pallas import tpu as pltpu
from jax.sharding import PartitionSpec as P

HD = 64
LANES = 256
PACK = 16
LOG2_E = 1.4426950408889634
MESH = pl.DeviceIdType.MESH


def fill_masks(head_mean, head_sum, head_rows, allowed, pg):
    heads = LANES // HD
    row = lax.broadcasted_iota(jnp.int32, (LANES, LANES), 0)
    column = lax.broadcasted_iota(jnp.int32, (LANES, LANES), 1)
    head_mean[...] = jnp.where(row // HD == column // HD, 1.0 / HD, 0.0).astype(jnp.bfloat16)
    few_columns = lax.broadcasted_iota(jnp.int32, (PACK, LANES), 1)
    for h in range(heads):
        across = (h + heads // 2) % heads
        head_sum[h] = jnp.where(few_columns // HD == across, 1.0, 0.0).astype(jnp.bfloat16)
        head_rows[h] = jnp.where(few_columns // HD == h, 1.0, 0.0).astype(jnp.bfloat16)
    allowed[...] = jnp.where(
        (lax.rem(row, pg) == lax.rem(column, pg)) & (row >= column), 1.0, 0.0
    ).astype(jnp.bfloat16)


def attend(x, gain, qkv_ref, out_ref, scale_ref, masks, allowed, normed, attn):
    head_mean, head_sum, head_rows = masks
    count, width = x.shape
    heads = LANES // HD
    square = jnp.mean(x * x, -1, keepdims=True)
    normed[...] = (x * lax.rsqrt(square + 1e-05) * gain).astype(jnp.bfloat16)
    lane_head = lax.broadcasted_iota(jnp.int32, (1, LANES), 1) // HD
    pair, split = heads // 2, LANES // 2

    def unit(part):
        mean = jnp.dot(
            (part * part).astype(jnp.bfloat16), head_mean[...], preferred_element_type=jnp.float32
        )
        return part * lax.rsqrt(mean + 1e-06)

    def by_head(part):
        return jnp.concatenate([part * head_rows[h][:1] for h in range(heads)], 0)

    def prepare(g):
        def project(block):
            first = block * width + g * LANES
            return jnp.dot(
                normed[...], qkv_ref[:, first : first + LANES], preferred_element_type=jnp.float32
            )

        scale = jnp.zeros((1, LANES), jnp.float32)
        for h in range(heads):
            scale = jnp.where(lane_head == h, scale_ref[g * heads + h], scale)
        query = (unit(project(0)) * (scale * (LOG2_E / HD))).astype(jnp.bfloat16)
        key = unit(project(1)).astype(jnp.bfloat16)
        value = project(2).astype(jnp.bfloat16)
        values = [
            jnp.concatenate(
                [value * head_rows[h][:1] + head_sum[h][:1] for h in range(first, first + pair)], 0
            )
            for first in range(0, heads, pair)
        ]
        return by_head(query), key, values

    ready = prepare(0)
    for g in range(width // LANES):
        stacked, key, values = ready
        scores = lax.dot_general(
            stacked, key, (((1,), (1,)), ((), ())), preferred_element_type=jnp.float32
        )
        if (g + 1) * LANES < width:
            ready = prepare(g + 1)
        weights = []
        for h in range(heads):
            weight = jnp.exp2(scores[h * count : (h + 1) * count]).astype(jnp.bfloat16)
            weights.append(weight if allowed is None else weight * allowed[...])
        low, high = (
            jnp.dot(
                jnp.concatenate(weights[first : first + pair], 1),
                values[first // pair],
                preferred_element_type=jnp.float32,
            )
            for first in (0, pair)
        )
        columns = g * LANES
        attn[:, columns : columns + split] = (low[:, :split] / low[:, split:]).astype(jnp.bfloat16)
        attn[:, columns + split : columns + LANES] = (high[:, split:] / high[:, :split]).astype(
            jnp.bfloat16
        )
    return x + jnp.dot(attn[...], out_ref[...], preferred_element_type=jnp.float32)


def kernel(
    n_tm,
    n_patch,
    x_hbm,
    codes_ref,
    gain_space,
    qkv_space_hbm,
    out_space_hbm,
    scale_space,
    gain_time,
    qkv_time_hbm,
    out_time_hbm,
    scale_time,
    codebook_hbm,
    encoded,
    commitment,
    qkv_space,
    out_space,
    qkv_time,
    out_time,
    codebook,
    whole,
    packed,
    arrived,
    wide,
    leaving,
    landed,
    chosen,
    normed_s,
    attn_s,
    normed_t,
    attn_t,
    head_mean,
    head_sum,
    head_rows,
    allowed,
    load_sem,
    in_send,
    in_recv,
    mid_send,
    mid_recv,
    out_send,
    out_recv,
):
    f_local, p_local, width = x_hbm.shape
    f_own, count = whole.shape[:2]
    halves, piece = arrived.shape[0], arrived.shape[3]
    pg = p_local // n_tm // halves
    pieces = PACK // pg
    n = n_tm * n_patch
    frames = f_local * n_tm
    i = lax.axis_index("tm")
    j = lax.axis_index("patch")
    me = j * n_tm + i

    barrier = pltpu.get_barrier_semaphore()

    def greet(k, carry):
        other = lax.rem(me + k, n)
        pl.semaphore_signal(
            barrier,
            inc=1,
            device_id=(lax.rem(other, n_tm), other // n_tm),
            device_id_type=MESH,
        )
        return carry

    lax.fori_loop(1, n, greet, 0)
    sources = (qkv_space_hbm, out_space_hbm, qkv_time_hbm, out_time_hbm, codebook_hbm)
    targets = (qkv_space, out_space, qkv_time, out_time, codebook)
    loads = [
        pltpu.make_async_copy(source, target, load_sem.at[k])
        for k, (source, target) in enumerate(zip(sources, targets))
    ]
    pl.semaphore_wait(barrier, n - 1)

    rows = pl.ds(pl.multiple_of(j * p_local, p_local), p_local)

    def share(f):
        for k in range(1, n_patch):
            to = lax.rem(j + k, n_patch)
            pltpu.make_async_remote_copy(
                src_ref=x_hbm.at[to * f_own + f],
                dst_ref=whole.at[f, rows],
                send_sem=in_send.at[f],
                recv_sem=in_recv.at[f],
                device_id=(i, to),
                device_id_type=MESH,
            ).start()
        pltpu.make_async_copy(x_hbm.at[j * f_own + f], whole.at[f, rows], in_recv.at[f]).start()

    def shared(f):
        sent = x_hbm.at[pl.ds(0, n_patch - 1)]
        pltpu.make_async_copy(sent, sent, in_send.at[f]).wait()

    share(0)
    for k in (4, 0, 1, 2, 3):
        loads[k].start()

    fill_masks(head_mean, head_sum, head_rows, allowed, pg)
    masks = (head_mean, head_sum, head_rows)
    loads[4].wait()
    code_columns = jnp.transpose(codes_ref[...].astype(jnp.float32))
    code_ids = lax.broadcasted_iota(jnp.int32, (p_local, codebook.shape[0]), 1).astype(jnp.float32)
    for f in range(f_local):
        one_hot = jnp.where(code_columns[:, f : f + 1] == code_ids, 1.0, 0.0).astype(jnp.bfloat16)
        chosen[f] = jnp.dot(
            one_hot, codebook[...], preferred_element_type=jnp.float32
        ).astype(jnp.bfloat16)

    loads[0].wait()
    loads[1].wait()
    for f in range(1, f_own):
        shared(f - 1)
        share(f)
    for f in range(f_own):
        pltpu.make_async_copy(whole.at[f], whole.at[f], in_recv.at[f]).wait()
        stream = attend(
            whole[f].astype(jnp.float32),
            gain_space[...],
            qkv_space,
            out_space,
            scale_space,
            masks,
            None,
            normed_s,
            attn_s,
        )
        blocks = stream.reshape(n * halves, pg, width)
        packed[f] = (
            jnp.concatenate([blocks[:, :, c * piece : (c + 1) * piece] for c in range(pieces)], 1)
            .astype(jnp.bfloat16)
            .reshape(packed.shape[1:])
        )
        frame = i * f_local + j * f_own + f
        last = f == f_own - 1

        def send(k, carry, half):
            other = lax.rem(me + k, n)
            to_i, to_j = lax.rem(other, n_tm), other // n_tm
            part = half if last else slice(None)
            pltpu.make_async_remote_copy(
                src_ref=packed.at[f, to_j, part, to_i],
                dst_ref=arrived.at[part, frame],
                send_sem=mid_send,
                recv_sem=mid_recv.at[half if last else halves],
                device_id=(to_i, to_j),
                device_id_type=MESH,
            ).start()
            return carry

        for half in range(halves if last else 1):
            part = half if last else slice(None)
            lax.fori_loop(1, n, functools.partial(send, half=half), 0)
            pltpu.make_async_copy(
                packed.at[f, j, part, i],
                arrived.at[part, frame],
                mid_recv.at[half if last else halves],
            ).start()

    loads[2].wait()
    loads[3].wait()
    if f_own > 1:
        early = arrived.at[:, pl.ds(0, (f_own - 1) * n)]
        pltpu.make_async_copy(early, early, mid_recv.at[halves]).wait()
    for half in range(halves):
        late = arrived.at[half, pl.ds(0, n)]
        pltpu.make_async_copy(late, late, mid_recv.at[half]).wait()
        for c in range(pieces):
            wide[:, c * piece : (c + 1) * piece] = (
                arrived[half, :, c * pg : (c + 1) * pg, :]
                .astype(jnp.float32)
                .reshape(LANES, piece)
            )
        result = attend(
            wide[...],
            gain_time[...],
            qkv_time,
            out_time,
            scale_time,
            masks,
            allowed,
            normed_t,
            attn_t,

        )
        leaving[half] = result.astype(jnp.bfloat16).reshape(leaving.shape[1:])

        def send_back(k, carry):
            to = lax.rem(i + k, n_tm)
            pltpu.make_async_remote_copy(
                src_ref=leaving.at[half, to],
                dst_ref=landed.at[half, i],
                send_sem=out_send,
                recv_sem=out_recv.at[half],
                device_id=(to, j),
                device_id_type=MESH,
            ).start()
            return carry

        lax.fori_loop(1, n_tm, send_back, 0)
        pltpu.make_async_copy(leaving.at[half, i], landed.at[half, i], out_recv.at[half]).start()

    for half in range(halves):
        pltpu.make_async_copy(landed.at[half], landed.at[half], out_recv.at[half]).wait()
        for first in range(0, n_tm, pieces):
            output = jnp.concatenate(
                [
                    landed[half, first + k].astype(jnp.float32).reshape(f_local, pg, width)
                    for k in range(pieces)
                ],
                1,
            )
            part = pl.ds(half * (p_local // halves) + first * pg, PACK)
            encoded[:, part, :] = output.astype(jnp.bfloat16)
            commitment[:, part, :] = (output - chosen[:, part, :].astype(jnp.float32)).astype(
                jnp.bfloat16
            )

    shared(f_own - 1)
    for f in range(f_own):
        sent = packed.at[f, pl.ds(0, n_patch - 1)]
        pltpu.make_async_copy(sent, sent, mid_send).wait()
        sent = packed.at[f, 0, :, pl.ds(0, n_tm - 1)]
        pltpu.make_async_copy(sent, sent, mid_send).wait()
    sent = leaving.at[:, pl.ds(0, n_tm - 1)]
    pltpu.make_async_copy(sent, sent, out_send).wait()


def solution(mesh):
    n_tm, n_patch = mesh.shape["tm"], mesh.shape["patch"]
    n = n_tm * n_patch

    def shards(x, codes, g_s, w_s, o_s, s_s, g_t, w_t, o_t, s_t, book):
        f_local, p_local, width = x.shape
        f_own, count = f_local // n_patch, p_local * n_patch
        frames = f_local * n_tm
        pg = max(1, LANES // frames)
        halves = p_local // n_tm // pg
        piece = width * pg // PACK
        any_space = pl.BlockSpec(memory_space=pl.ANY)
        vmem = pl.BlockSpec(memory_space=pltpu.VMEM)
        smem = pl.BlockSpec(memory_space=pltpu.SMEM)
        bf16, f32 = jnp.bfloat16, jnp.float32
        return pl.pallas_call(
            functools.partial(kernel, n_tm, n_patch),
            out_shape=[jax.ShapeDtypeStruct(x.shape, bf16)] * 2,
            in_specs=[
                any_space,
                vmem,
                vmem,
                any_space,
                any_space,
                smem,
                vmem,
                any_space,
                any_space,
                smem,
                any_space,
            ],
            out_specs=[vmem, vmem],
            scratch_shapes=[
                pltpu.VMEM(w_s.shape, bf16),
                pltpu.VMEM(o_s.shape, bf16),
                pltpu.VMEM(w_t.shape, bf16),
                pltpu.VMEM(o_t.shape, bf16),
                pltpu.VMEM(book.shape, bf16),
                pltpu.VMEM((f_own, count, width), bf16),
                pltpu.VMEM((f_own, n_patch, halves, n_tm, PACK, piece), bf16),
                pltpu.VMEM((halves, frames, PACK, piece), bf16),
                pltpu.VMEM((LANES, width), f32),
                pltpu.VMEM((halves, n_tm, f_local * pg, width), bf16),
                pltpu.VMEM((halves, n_tm, f_local * pg, width), bf16),
                pltpu.VMEM(x.shape, bf16),
                pltpu.VMEM((count, width), bf16),
                pltpu.VMEM((count, width), bf16),
                pltpu.VMEM((LANES, width), bf16),
                pltpu.VMEM((LANES, width), bf16),
                pltpu.VMEM((LANES, LANES), bf16),
                pltpu.VMEM((LANES // HD, PACK, LANES), bf16),
                pltpu.VMEM((LANES // HD, PACK, LANES), bf16),
                pltpu.VMEM((LANES, LANES), bf16),
                pltpu.SemaphoreType.DMA((5,)),
                pltpu.SemaphoreType.DMA((f_own,)),
                pltpu.SemaphoreType.DMA((f_own,)),
                pltpu.SemaphoreType.DMA,
                pltpu.SemaphoreType.DMA((halves + 1,)),
                pltpu.SemaphoreType.DMA,
                pltpu.SemaphoreType.DMA((halves,)),
            ],
            compiler_params=pltpu.CompilerParams(
                collective_id=0, has_side_effects=True, vmem_limit_bytes=56 * 1024 * 1024
            ),
            cost_estimate=pl.CostEstimate(
                flops=12_000_000_000, bytes_accessed=24_000_000, transcendentals=4_000_000
            ),
        )(
            x,
            codes,
            g_s.reshape(1, -1),
            w_s,
            o_s,
            s_s,
            g_t.reshape(1, -1),
            w_t,
            o_t,
            s_t,
            book,
        )

    return jax.shard_map(
        shards,
        mesh=mesh,
        in_specs=(P("tm", "patch", None), P("tm", "patch")) + (P(),) * 9,
        out_specs=(P("tm", "patch", None), P("tm", "patch", None)),
        check_vma=False,
    )
```
